512 devices in a mesh: aux: 32 (over z_lo, y), row: 4 (over x), col: 4 (over z_hi, core).
Axes of the slice: x: 4, y: 4, z: 16 (z_hi: 2, z_lo: 8; z = z_hi * 8 + z_lo), core: 2. Of those that a mesh axis runs over, the one named last changes fastest.
Arguments:
- g_plus: bfloat16 [2048, 2048], P('row', ('aux', 'col')), may hold values from -0.125 to 0.125
- g_minus: bfloat16 [2048, 2048], P(('aux', 'row'), 'col'), may hold values from -0.125 to 0.125
- coulomb: bfloat16 [64, 2048, 2048], P('aux', 'row'), may hold values from -3 to 3
Outputs:
- sigma: bfloat16 [2048, 2048], P('row', 'col')
The draws below stay inside these ranges and needn't reach their ends.
All inputs are finite; a program needn't handle non-finite values.
Results may differ from the reference program's by a relative error of at most 0.0057.
Values may be sent and summed in bfloat16 or wider, within the bound.
No kernel may reach another device: no remote copies, remote signals or barrier semaphores. Data moves between devices by JAX's collectives and lax.ppermute only.
A program may use at most 64 MiB of HBM per device.

```python
import jax
import jax.numpy as jnp
from jax import lax

N = 2048
QS = 64


def block_scale(stream_key, shape, cuts, smallest, high):
    def one(position, blocks):
        draws = jax.random.uniform(jax.random.fold_in(jax.random.fold_in(stream_key, 6), position), (blocks,), jnp.float32, smallest / len(cuts), high / len(cuts))
        return jnp.repeat(jnp.exp(draws), shape[position] // blocks).reshape((-1,) + (1,) * (len(shape) - position - 1))

    level = one(*cuts[0])
    for cut in cuts[1:]:
        level = level * one(*cut)
    return level


def noise(rng, dims, width, most, pieces=(), held_as=jnp.bfloat16):
    array = width * jax.random.normal(rng, dims, jnp.float32)
    if pieces:
        array = array * block_scale(rng, dims, pieces, -0.22, 0.18)
    return jnp.clip(array, -most, most).astype(held_as)


def setup_inputs(seed: int = 0) -> dict:
    key_list = jax.random.split(jax.random.key(seed), 4)
    g_plus = noise(key_list[0], (N, N), N ** -0.5, 0.125, ((0, 4), (1, 128)))
    g_minus = noise(key_list[1], (N, N), N ** -0.5, 0.125, ((0, 128), (1, 4)))
    coulomb = noise(key_list[2], (QS, N, N), 0.5, 3.0, ((0, 32), (1, 4)))
    return {"g_plus": g_plus, "g_minus": g_minus, "coulomb": coulomb}


def reference(g_plus, g_minus, coulomb):
    def step(index, total):
        matrix = lax.dynamic_index_in_dim(coulomb, index, 0, keepdims=False)
        half = jnp.dot(matrix, g_minus, preferred_element_type=jnp.float32).astype(jnp.bfloat16)
        pair = jnp.dot(g_plus, half, preferred_element_type=jnp.float32)
        return total + pair * half.astype(jnp.float32)

    total = lax.fori_loop(0, QS, step, jnp.zeros((N, N), jnp.float32))
    return (-total).astype(jnp.bfloat16)
```

```python
import jax
import jax.numpy as jnp
from jax import lax
from jax.sharding import Mesh, PartitionSpec as P

BF = jnp.bfloat16
F32 = jnp.float32


def spread(block, axes, count):
    return lax.all_to_all(jnp.broadcast_to(block[None], (count,) + block.shape), axes, 0, 0)


def shift(count, by):
    return [(index, (index + by) % count) for index in range(count)]


def solution(mesh):
    aux, row, col = (mesh.shape[name] for name in ("aux", "row", "col"))
    zl, y, zh, core = aux // 4, 4, col // 2, 2
    fine = Mesh(mesh.devices.reshape(zl, y, row, zh, core), ("zl", "y", "row", "zh", "core"))

    def local(g_plus, g_minus, coulomb):
        count, rows, n = coulomb.shape
        cols = g_minus.shape[1]
        depth = g_minus.shape[0]
        minus = spread(g_minus, "zl", zl)
        minus = spread(minus, ("y", "row"), y * row)
        minus = minus.reshape(y, row, zl, depth, cols).transpose(2, 0, 1, 3, 4).reshape(n, cols)
        thin = g_plus.shape[1]
        plus = spread(g_plus.T, ("zl", "zh"), zl * zh)
        plus = spread(plus, "y", y)
        plus = spread(plus, "core", core)
        plus = plus.reshape(core, y, zl, zh, thin, rows).transpose(2, 1, 3, 0, 4, 5).reshape(n, rows)

        half = jnp.einsum("qik,kj->qij", coulomb, minus, preferred_element_type=F32).astype(BF)

        me = lax.axis_index("row")
        left = lax.ppermute(half, "row", shift(row, 1))
        right = lax.ppermute(half, "row", shift(row, -1))
        cut = rows // 2
        top = lax.ppermute(left[:, :cut], "row", shift(row, 1))
        bottom = lax.ppermute(right[:, cut:], "row", shift(row, -1))

        def part(strip, owner, start):
            size = strip.shape[1]
            block = lax.dynamic_slice_in_dim(plus, owner * rows + start, size, axis=0)
            return jnp.einsum("ki,qkj->qij", block, strip, preferred_element_type=F32)

        pair = part(half, me, 0)
        pair += part(left, (me + row - 1) % row, 0)
        pair += part(right, (me + 1) % row, 0)
        pair += part(top, (me + 2) % row, 0)
        pair += part(bottom, (me + 2) % row, cut)
        total = jnp.sum(pair * half.astype(F32), axis=0)

        total = lax.all_to_all(total.astype(BF).reshape(y, rows // y, cols), "y", 0, 0)
        total = jnp.sum(total.astype(F32), axis=0)
        total = lax.all_to_all(total.astype(BF).reshape(zl, rows // y // zl, cols), "zl", 0, 0)
        total = -jnp.sum(total.astype(F32), axis=0)
        whole = spread(total.astype(BF), "zl", zl)
        whole = spread(whole, "y", y)
        return whole.reshape(rows, cols)

    in_specs = (
        P("row", ("zl", "y", "zh", "core")),
        P(("zl", "y", "row"), ("zh", "core")),
        P(("zl", "y"), "row", None),
    )
    out_specs = P("row", ("zh", "core"))
    return jax.shard_map(local, mesh=fine, in_specs=in_specs, out_specs=out_specs, check_vma=False)
```

```python
import jax
import jax.numpy as jnp
from jax import lax
from jax.sharding import Mesh, PartitionSpec as P

BF = jnp.bfloat16
F32 = jnp.float32


def spread(block, axes, count):
    return lax.all_to_all(jnp.broadcast_to(block[None], (count,) + block.shape), axes, 0, 0)


def shift(count, by):
    return [(index, (index + by) % count) for index in range(count)]


def solution(mesh):
    aux, row, col = (mesh.shape[name] for name in ("aux", "row", "col"))
    zl, y, zh, core = aux // 4, 4, col // 2, 2
    fine = Mesh(mesh.devices.reshape(zl, y, row, zh, core), ("zl", "y", "row", "zh", "core"))

    def local(g_plus, g_minus, coulomb):
        count, rows, n = coulomb.shape
        cols = g_minus.shape[1]
        depth = g_minus.shape[0]
        minus = spread(g_minus, "zl", zl)
        minus = spread(minus, ("y", "row"), y * row)
        minus = minus.reshape(y, row, zl, depth, cols).transpose(2, 0, 1, 3, 4).reshape(n, cols)
        half = jnp.einsum("qik,kj->qij", coulomb, minus, preferred_element_type=F32).astype(BF)

        thin = g_plus.shape[1]
        plus = lax.all_gather(g_plus.T, ("zl", "zh"), axis=0, tiled=True)
        plus, later = lax.optimization_barrier((plus, half))
        plus = spread(plus, "y", y)
        plus = spread(plus, "core", core)
        plus = plus.reshape(core, y, zl, zh, thin, rows).transpose(2, 1, 3, 0, 4, 5).reshape(n, rows)

        me = lax.axis_index("row")
        left = lax.ppermute(half, "row", shift(row, 1))
        right = lax.ppermute(half, "row", shift(row, -1))
        cut = rows // 2
        top = lax.ppermute(left[:, :cut], "row", shift(row, 1))
        bottom = lax.ppermute(right[:, cut:], "row", shift(row, -1))

        def part(strip, owner, start):
            size = strip.shape[1]
            block = lax.dynamic_slice_in_dim(plus, owner * rows + start, size, axis=0)
            return jnp.einsum("ki,qkj->qij", block, strip, preferred_element_type=F32)

        pair = part(half, me, 0)
        pair += part(left, (me + row - 1) % row, 0)
        pair += part(right, (me + 1) % row, 0)
        pair += part(top, (me + 2) % row, 0)
        pair += part(bottom, (me + 2) % row, cut)
        total = jnp.sum(pair * later.astype(F32), axis=0)

        total = lax.all_to_all(total.astype(BF).reshape(y, rows // y, cols), "y", 0, 0)
        total = jnp.sum(total.astype(F32), axis=0)
        total = lax.all_to_all(total.astype(BF).reshape(zl, rows // y // zl, cols), "zl", 0, 0)
        total = -jnp.sum(total.astype(F32), axis=0)
        whole = spread(total.astype(BF), "zl", zl)
        whole = spread(whole, "y", y)
        return whole.reshape(rows, cols)

    in_specs = (
        P("row", ("zl", "y", "zh", "core")),
        P(("zl", "y", "row"), ("zh", "core")),
        P(("zl", "y"), "row", None),
    )
    out_specs = P("row", ("zh", "core"))
    return jax.shard_map(local, mesh=fine, in_specs=in_specs, out_specs=out_specs, check_vma=False)
```

```python
import jax
import jax.numpy as jnp
from jax import lax
from jax.sharding import Mesh, PartitionSpec as P

BF = jnp.bfloat16
F32 = jnp.float32


def spread(block, axes, count):
    return lax.all_to_all(jnp.broadcast_to(block[None], (count,) + block.shape), axes, 0, 0)


def shift(count, by):
    return [(index, (index + by) % count) for index in range(count)]


def partner(block, axis):
    return lax.ppermute(block, axis, shift(2, 1))


def order(mine, theirs, axis):
    first = lax.axis_index(axis) == 0
    return jnp.stack([jnp.where(first, mine, theirs), jnp.where(first, theirs, mine)])


def solution(mesh):
    aux, row, col = (mesh.shape[name] for name in ("aux", "row", "col"))
    zl, y, zh, core = aux // 4, 4, col // 2, 2
    fine = Mesh(mesh.devices.reshape(zl, y, row, zh, core), ("zl", "y", "row", "zh", "core"))

    def local(g_plus, g_minus, coulomb):
        count, rows, n = coulomb.shape
        depth, cols = g_minus.shape
        thin = g_plus.shape[1]
        slabs = spread(jnp.concatenate([g_minus, g_plus.T]), "zl", zl)
        minus, plus = slabs[:, :depth], slabs[:, depth:]
        theirs = partner(plus, "zh")
        minus = spread(minus, ("y", "row"), y * row)
        minus = minus.reshape(y, row, zl, depth, cols).transpose(2, 0, 1, 3, 4).reshape(n, cols)
        half = jnp.einsum("qik,kj->qij", coulomb, minus, preferred_element_type=F32).astype(BF)

        plus, theirs, later = lax.optimization_barrier((plus, theirs, half))
        plus = spread(order(plus, theirs, "zh"), "y", y)
        plus = order(plus, partner(plus, "core"), "core")
        plus = plus.reshape(core, y, zh, zl, thin, rows).transpose(3, 1, 2, 0, 4, 5).reshape(n, rows)

        me = lax.axis_index("row")
        left = lax.ppermute(half, "row", shift(row, 1))
        right = lax.ppermute(half, "row", shift(row, -1))
        cut = rows // 2
        top = lax.ppermute(left[:, :cut], "row", shift(row, 1))
        bottom = lax.ppermute(right[:, cut:], "row", shift(row, -1))

        def part(strip, owner, start):
            size = strip.shape[1]
            block = lax.dynamic_slice_in_dim(plus, owner * rows + start, size, axis=0)
            return jnp.einsum("ki,qkj->qij", block, strip, preferred_element_type=F32)

        pair = part(half, me, 0)
        pair += part(left, (me + row - 1) % row, 0)
        pair += part(right, (me + 1) % row, 0)
        pair += part(top, (me + 2) % row, 0)
        pair += part(bottom, (me + 2) % row, cut)
        total = jnp.sum(pair * later.astype(F32), axis=0)

        total = lax.all_to_all(total.astype(BF).reshape(y, rows // y, cols), "y", 0, 0)
        total = jnp.sum(total.astype(F32), axis=0)
        total = lax.all_to_all(total.astype(BF).reshape(zl, rows // y // zl, cols), "zl", 0, 0)
        total = -jnp.sum(total.astype(F32), axis=0)
        whole = spread(total.astype(BF), "zl", zl)
        whole = spread(whole, "y", y)
        return whole.reshape(rows, cols)

    in_specs = (
        P("row", ("zl", "y", "zh", "core")),
        P(("zl", "y", "row"), ("zh", "core")),
        P(("zl", "y"), "row", None),
    )
    out_specs = P("row", ("zh", "core"))
    return jax.shard_map(local, mesh=fine, in_specs=in_specs, out_specs=out_specs, check_vma=False)
```

```python
import jax
import jax.numpy as jnp
from jax import lax
from jax.sharding import Mesh, PartitionSpec as P

BF = jnp.bfloat16
F32 = jnp.float32


def spread(block, axes, count):
    return lax.all_to_all(jnp.broadcast_to(block[None], (count,) + block.shape), axes, 0, 0)


def shift(count, by):
    return [(index, (index + by) % count) for index in range(count)]


def partner(block, axis):
    return lax.ppermute(block, axis, shift(2, 1))


def order(mine, theirs, axis):
    first = lax.axis_index(axis) == 0
    return jnp.stack([jnp.where(first, mine, theirs), jnp.where(first, theirs, mine)])


def solution(mesh):
    aux, row, col = (mesh.shape[name] for name in ("aux", "row", "col"))
    zl, y, zh, core = aux // 4, 4, col // 2, 2
    fine = Mesh(mesh.devices.reshape(zl, y, row, zh, core), ("zl", "y", "row", "zh", "core"))

    def local(g_plus, g_minus, coulomb):
        count, rows, n = coulomb.shape
        depth, cols = g_minus.shape
        thin = g_plus.shape[1]
        slabs = spread(jnp.concatenate([g_minus, g_plus.T]), "zl", zl)
        minus, plus = slabs[:, :depth], slabs[:, depth:]
        theirs = partner(plus, "zh")
        minus = spread(minus, ("y", "row"), y * row)
        minus = minus.reshape(y, row, zl, depth, cols).transpose(2, 0, 1, 3, 4).reshape(n, cols)
        half = jnp.einsum("qik,kj->qij", coulomb, minus, preferred_element_type=F32).astype(BF)

        plus, theirs, later = lax.optimization_barrier((plus, theirs, half))
        plus = spread(order(plus, theirs, "zh"), "y", y)
        left = lax.ppermute(half, "row", shift(row, 1))
        right = lax.ppermute(half, "row", shift(row, -1))
        plus, left, right = lax.optimization_barrier((plus, left, right))
        plus = order(plus, partner(plus, "core"), "core")
        plus = plus.reshape(core, y, zh, zl, thin, rows).transpose(3, 1, 2, 0, 4, 5).reshape(n, rows)

        me = lax.axis_index("row")
        far0 = lax.ppermute(left[0], "row", shift(row, 1))
        far1 = lax.ppermute(right[1], "row", shift(row, -1))

        def block(owner):
            return lax.dynamic_slice_in_dim(plus, owner % row * rows, rows, axis=0)

        def part(owner, *strips):
            factor = block(owner)
            return [jnp.einsum("ki,kj->ij", factor, strip, preferred_element_type=F32) for strip in strips]

        parts = [part(me, *half), part(me + row - 1, *left), part(me + 1, *right), part(me + 2, far0, far1)]
        pair0, pair1 = (sum(piece[index] for piece in parts) for index in (0, 1))
        total = pair0 * later[0].astype(F32) + pair1 * later[1].astype(F32)

        total = lax.all_to_all(total.astype(BF).reshape(y, rows // y, cols), "y", 0, 0)
        total = jnp.sum(total.astype(F32), axis=0)
        total = lax.all_to_all(total.astype(BF).reshape(zl, rows // y // zl, cols), "zl", 0, 0)
        total = -jnp.sum(total.astype(F32), axis=0)
        whole = spread(total.astype(BF), "zl", zl)
        whole = spread(whole, "y", y)
        return whole.reshape(rows, cols)

    in_specs = (
        P("row", ("zl", "y", "zh", "core")),
        P(("zl", "y", "row"), ("zh", "core")),
        P(("zl", "y"), "row", None),
    )
    out_specs = P("row", ("zh", "core"))
    return jax.shard_map(local, mesh=fine, in_specs=in_specs, out_specs=out_specs, check_vma=False)
```

```python
import jax
import jax.numpy as jnp
from jax import lax
from jax.sharding import Mesh, PartitionSpec as P

BF = jnp.bfloat16
F32 = jnp.float32


def spread(block, axes, count):
    return lax.all_to_all(jnp.broadcast_to(block[None], (count,) + block.shape), axes, 0, 0)


def shift(count, by):
    return [(index, (index + by) % count) for index in range(count)]


def partner(block, axis):
    return lax.ppermute(block, axis, shift(2, 1))


def order(mine, theirs, axis):
    first = lax.axis_index(axis) == 0
    return jnp.stack([jnp.where(first, mine, theirs), jnp.where(first, theirs, mine)])


def solution(mesh):
    aux, row, col = (mesh.shape[name] for name in ("aux", "row", "col"))
    zl, y, zh, core = aux // 4, 4, col // 2, 2
    fine = Mesh(mesh.devices.reshape(zl, y, row, zh, core), ("zl", "y", "row", "zh", "core"))

    def local(g_plus, g_minus, coulomb):
        count, rows, n = coulomb.shape
        depth, cols = g_minus.shape
        thin = g_plus.shape[1]
        slabs = spread(jnp.concatenate([g_minus, g_plus.T]), "zl", zl)
        minus, plus = slabs[:, :depth], slabs[:, depth:]
        theirs = partner(plus, "zh")
        minus = spread(minus, ("y", "row"), y * row)
        minus, plus, theirs = lax.optimization_barrier((minus, plus, theirs))
        plus = order(plus, theirs, "zh")
        theirs = partner(plus, "core")
        minus = minus.reshape(y, row, zl, depth, cols).transpose(2, 0, 1, 3, 4).reshape(n, cols)
        q0, q1 = (jnp.dot(coulomb[q], minus, preferred_element_type=F32).astype(BF) for q in (0, 1))

        left0 = lax.ppermute(q0, "row", shift(row, 1))
        right1 = lax.ppermute(q1, "row", shift(row, -1))
        left1 = lax.ppermute(q1, "row", shift(row, 1))
        right0 = lax.ppermute(q0, "row", shift(row, -1))
        far0 = lax.ppermute(left0, "row", shift(row, 1))
        far1 = lax.ppermute(right1, "row", shift(row, -1))

        plus, theirs, later0, later1 = lax.optimization_barrier((plus, theirs, q0, q1))
        plus = spread(order(plus, theirs, "core"), "y", y)
        plus, left1, right0 = lax.optimization_barrier((plus, left1, right0))
        plus = plus.reshape(y, core, zh, zl, thin, rows).transpose(3, 0, 2, 1, 4, 5).reshape(n, rows)

        me = lax.axis_index("row")

        def block(owner):
            return lax.dynamic_slice_in_dim(plus, owner % row * rows, rows, axis=0)

        def part(owner, *strips):
            factor = block(owner)
            return [jnp.einsum("ki,kj->ij", factor, strip, preferred_element_type=F32) for strip in strips]

        parts = [part(me, q0, q1), part(me + row - 1, left0, left1), part(me + 1, right0, right1), part(me + 2, far0, far1)]
        pair0, pair1 = (sum(piece[index] for piece in parts) for index in (0, 1))
        total = pair0 * later0.astype(F32) + pair1 * later1.astype(F32)

        total = lax.all_to_all(total.astype(BF).reshape(y, rows // y, cols), "y", 0, 0)
        total = jnp.sum(total.astype(F32), axis=0)
        total = lax.all_to_all(total.astype(BF).reshape(zl, rows // y // zl, cols), "zl", 0, 0)
        total = -jnp.sum(total.astype(F32), axis=0)
        whole = spread(total.astype(BF), "zl", zl)
        whole = spread(whole, "y", y)
        return whole.reshape(rows, cols)

    in_specs = (
        P("row", ("zl", "y", "zh", "core")),
        P(("zl", "y", "row"), ("zh", "core")),
        P(("zl", "y"), "row", None),
    )
    out_specs = P("row", ("zh", "core"))
    return jax.shard_map(local, mesh=fine, in_specs=in_specs, out_specs=out_specs, check_vma=False)
```

```python
import jax
import jax.numpy as jnp
from jax import lax
from jax.sharding import Mesh, PartitionSpec as P

BF = jnp.bfloat16
F32 = jnp.float32


def spread(block, axes, count):
    return lax.all_to_all(jnp.broadcast_to(block[None], (count,) + block.shape), axes, 0, 0)


def shift(count, by):
    return [(index, (index + by) % count) for index in range(count)]


def partner(block, axis):
    return lax.ppermute(block, axis, shift(2, 1))


def order(mine, theirs, axis):
    first = lax.axis_index(axis) == 0
    return jnp.stack([jnp.where(first, mine, theirs), jnp.where(first, theirs, mine)])


def solution(mesh):
    aux, row, col = (mesh.shape[name] for name in ("aux", "row", "col"))
    z2, z1, y, zh, core = 2, aux // 8, 4, col // 2, 2
    zl = z2 * z1
    names = ("z2", "z1", "y", "row", "zh", "core")
    fine = Mesh(mesh.devices.reshape(z2, z1, y, row, zh, core), names)
    line = ("z2", "z1")

    def local(g_plus, g_minus, coulomb):
        count, rows, n = coulomb.shape
        depth, cols = g_minus.shape
        thin = g_plus.shape[1]
        slabs = spread(jnp.concatenate([g_minus, g_plus.T]), line, zl)
        minus, plus = slabs[:, :depth], slabs[:, depth:]
        theirs = partner(plus, "zh")
        minus = spread(minus, ("y", "row"), y * row)
        minus, plus, theirs = lax.optimization_barrier((minus, plus, theirs))
        plus = order(plus, theirs, "zh")
        theirs = partner(plus, "core")
        minus = minus.reshape(y, row, zl, depth, cols).transpose(2, 0, 1, 3, 4).reshape(n, cols)
        q0, q1 = (jnp.dot(coulomb[q], minus, preferred_element_type=F32).astype(BF) for q in (0, 1))

        left0 = lax.ppermute(q0, "row", shift(row, 1))
        right1 = lax.ppermute(q1, "row", shift(row, -1))
        left1 = lax.ppermute(q1, "row", shift(row, 1))
        right0 = lax.ppermute(q0, "row", shift(row, -1))
        far0 = lax.ppermute(left0, "row", shift(row, 1))
        far1 = lax.ppermute(right1, "row", shift(row, -1))

        plus, theirs, later0, later1 = lax.optimization_barrier((plus, theirs, q0, q1))
        plus = spread(order(plus, theirs, "core"), "y", y)
        plus, left1, right0 = lax.optimization_barrier((plus, left1, right0))
        plus = plus.reshape(y, core, zh, zl, thin, rows).transpose(3, 0, 2, 1, 4, 5).reshape(n, rows)

        me = lax.axis_index("row")

        def block(owner):
            return lax.dynamic_slice_in_dim(plus, owner % row * rows, rows, axis=0)

        def part(owner, *strips):
            factor = block(owner)
            return [jnp.einsum("ki,kj->ij", factor, strip, preferred_element_type=F32) for strip in strips]

        parts = [part(me, q0, q1), part(me + row - 1, left0, left1), part(me + 1, right0, right1), part(me + 2, far0, far1)]
        pair0, pair1 = (sum(piece[index] for piece in parts) for index in (0, 1))
        total = pair0 * later0.astype(F32) + pair1 * later1.astype(F32)

        parts = y * z1
        total = lax.all_to_all(total.astype(BF).reshape(parts, rows // parts, cols), ("y", "z1"), 0, 0)
        total = jnp.sum(total.astype(F32), axis=0)
        total = -(total + partner(total, "z2"))
        return spread(total.astype(BF), ("y", "z1"), parts).reshape(rows, cols)

    in_specs = (
        P("row", ("z2", "z1", "y", "zh", "core")),
        P(("z2", "z1", "y", "row"), ("zh", "core")),
        P(("z2", "z1", "y"), "row", None),
    )
    out_specs = P("row", ("zh", "core"))
    return jax.shard_map(local, mesh=fine, in_specs=in_specs, out_specs=out_specs, check_vma=False)
```

```python
import jax
import jax.numpy as jnp
import numpy as np
from jax import lax
from jax.sharding import Mesh, PartitionSpec as P

BF = jnp.bfloat16
F32 = jnp.float32


def spread(block, axes, count):
    return lax.all_to_all(jnp.broadcast_to(block[None], (count,) + block.shape), axes, 0, 0)


def shift(count, by):
    return [(index, (index + by) % count) for index in range(count)]


def partner(block, axis):
    return lax.ppermute(block, axis, shift(2, 1))


def solution(mesh):
    aux, row, col = (mesh.shape[name] for name in ("aux", "row", "col"))
    z2, z1, y, zh, core = 2, aux // 8, 4, col // 2, 2
    zl = z2 * z1
    names = ("z2", "z1", "y", "row", "zh", "core")
    fine = Mesh(mesh.devices.reshape(z2, z1, y, row, zh, core), names)
    line = ("z2", "z1")

    def local(g_plus, g_minus, coulomb):
        count, rows, n = coulomb.shape
        depth, cols = g_minus.shape
        thin = g_plus.shape[1]
        me = lax.axis_index("row").astype(jnp.uint32)
        starts = [(me + step) % row * rows for step in range(row)]
        first = lax.axis_index("core") == 0
        lower = lax.axis_index("zh") == 0

        plus = g_plus.T
        theirs = partner(plus, "zh")
        slab = jnp.concatenate([g_minus, jnp.where(lower, plus, theirs), jnp.where(lower, theirs, plus)])
        slab, first, *starts = lax.optimization_barrier((slab, first, *starts))
        slabs = spread(slab, line, zl)
        minus, plus = slabs[:, :depth], slabs[:, depth:]

        minus = spread(minus, ("y", "row"), y * row)
        minus = minus.reshape(y, row, zl, depth, cols).transpose(2, 0, 1, 3, 4).reshape(n, cols)
        half = jnp.einsum("qik,kj->qij", coulomb, minus, preferred_element_type=F32).astype(BF)

        left = lax.ppermute(half, "row", shift(row, 1))
        right = lax.ppermute(half, "row", shift(row, -1))
        far0 = lax.ppermute(left[0], "row", shift(row, 1))
        far1 = lax.ppermute(right[1], "row", shift(row, -1))

        plus, later = lax.optimization_barrier((plus, half))
        plus = spread(plus, "y", y)
        plus, left, right = lax.optimization_barrier((plus, left, right))
        theirs = partner(plus, "core")
        plus = jnp.stack([jnp.where(first, plus, theirs), jnp.where(first, theirs, plus)])
        plus = plus.reshape(core, y, zl, zh, thin, rows).transpose(2, 1, 3, 0, 4, 5).reshape(n, rows)

        def part(step, *strips):
            factor = lax.dynamic_slice(plus, (starts[step], np.uint32(0)), (rows, rows))
            return [jnp.einsum("ki,kj->ij", factor, strip, preferred_element_type=F32) for strip in strips]

        parts = [part(0, *half), part(row - 1, *left), part(1, *right), part(2, far0, far1)]
        pair0, pair1 = (sum(piece[index] for piece in parts) for index in (0, 1))
        total = pair0 * later[0].astype(F32) + pair1 * later[1].astype(F32)

        for axis, size in (("y", y), ("z1", z1)):
            total = total.astype(BF).reshape(size, -1, cols)
            total = jnp.sum(lax.all_to_all(total, axis, 0, 0).astype(F32), axis=0)
        total = -(total + partner(total, "z2"))
        whole = spread(spread(total.astype(BF), "z1", z1), "y", y)
        return whole.reshape(rows, cols)

    in_specs = (
        P("row", ("z2", "z1", "y", "zh", "core")),
        P(("z2", "z1", "y", "row"), ("zh", "core")),
        P(("z2", "z1", "y"), "row", None),
    )
    out_specs = P("row", ("zh", "core"))
    return jax.shard_map(local, mesh=fine, in_specs=in_specs, out_specs=out_specs, check_vma=False)
```

```python
import jax
import jax.numpy as jnp
from jax import lax
from jax.sharding import Mesh, PartitionSpec as P

BF = jnp.bfloat16
F32 = jnp.float32


def spread(block, axes, count):
    return lax.all_to_all(jnp.broadcast_to(block[None], (count,) + block.shape), axes, 0, 0)


def shift(count, by):
    return [(index, (index + by) % count) for index in range(count)]


def partner(block, axis):
    return lax.ppermute(block, axis, shift(2, 1))


def order(mine, theirs, axis):
    first = lax.axis_index(axis) == 0
    return jnp.stack([jnp.where(first, mine, theirs), jnp.where(first, theirs, mine)])


def solution(mesh):
    aux, row, col = (mesh.shape[name] for name in ("aux", "row", "col"))
    z2, z1, y, zh, core = 2, aux // 8, 4, col // 2, 2
    zl = z2 * z1
    names = ("z2", "z1", "y", "row", "zh", "core")
    fine = Mesh(mesh.devices.reshape(z2, z1, y, row, zh, core), names)
    line = ("z2", "z1")

    def local(g_plus, g_minus, coulomb):
        count, rows, n = coulomb.shape
        depth, cols = g_minus.shape
        thin = g_plus.shape[1]
        slabs = spread(jnp.concatenate([g_minus, g_plus.T]), line, zl)
        minus, plus = slabs[:, :depth], slabs[:, depth:]
        theirs = partner(plus, "zh")
        minus = spread(minus, ("y", "row"), y * row)
        minus, plus, theirs = lax.optimization_barrier((minus, plus, theirs))
        plus = order(plus, theirs, "zh")
        theirs = partner(plus, "core")
        minus = minus.reshape(y, row, zl, depth, cols).transpose(2, 0, 1, 3, 4).reshape(n, cols)
        q0, q1 = (jnp.dot(coulomb[q], minus, preferred_element_type=F32).astype(BF) for q in (0, 1))

        left0 = lax.ppermute(q0, "row", shift(row, 1))
        right1 = lax.ppermute(q1, "row", shift(row, -1))
        left1 = lax.ppermute(q1, "row", shift(row, 1))
        right0 = lax.ppermute(q0, "row", shift(row, -1))
        far0 = lax.ppermute(left0, "row", shift(row, 1))
        far1 = lax.ppermute(right1, "row", shift(row, -1))

        plus, theirs, later0, later1 = lax.optimization_barrier((plus, theirs, q0, q1))
        plus = order(plus, theirs, "core")
        ring = jnp.stack([plus] + [lax.ppermute(plus, "y", shift(y, step)) for step in range(1, y)])
        mine = lax.axis_index("y")
        plus = jnp.stack([lax.dynamic_index_in_dim(ring, (mine - at) % y, 0, keepdims=False) for at in range(y)])
        plus = plus.reshape(y, core, zh, zl, thin, rows).transpose(3, 0, 2, 1, 4, 5).reshape(n, rows)

        me = lax.axis_index("row")

        def block(owner):
            return lax.dynamic_slice_in_dim(plus, owner % row * rows, rows, axis=0)

        def part(owner, *strips):
            factor = block(owner)
            return [jnp.einsum("ki,kj->ij", factor, strip, preferred_element_type=F32) for strip in strips]

        parts = [part(me, q0, q1), part(me + row - 1, left0, left1), part(me + 1, right0, right1), part(me + 2, far0, far1)]
        pair0, pair1 = (sum(piece[index] for piece in parts) for index in (0, 1))
        total = pair0 * later0.astype(F32) + pair1 * later1.astype(F32)

        parts = y * z1
        total = lax.all_to_all(total.astype(BF).reshape(parts, rows // parts, cols), ("y", "z1"), 0, 0)
        total = jnp.sum(total.astype(F32), axis=0)
        total = -(total + partner(total, "z2"))
        return spread(total.astype(BF), ("y", "z1"), parts).reshape(rows, cols)

    in_specs = (
        P("row", ("z2", "z1", "y", "zh", "core")),
        P(("z2", "z1", "y", "row"), ("zh", "core")),
        P(("z2", "z1", "y"), "row", None),
    )
    out_specs = P("row", ("zh", "core"))
    return jax.shard_map(local, mesh=fine, in_specs=in_specs, out_specs=out_specs, check_vma=False)
```

```python
import jax
import jax.numpy as jnp
from jax import lax
from jax.experimental.layout import Layout, with_layout_constraint
from jax.sharding import Mesh, PartitionSpec as P

BF = jnp.bfloat16
F32 = jnp.float32


def spread(block, axes, count):
    return lax.all_to_all(jnp.broadcast_to(block[None], (count,) + block.shape), axes, 0, 0)


def shift(count, by):
    return [(index, (index + by) % count) for index in range(count)]


def partner(block, axis):
    return lax.ppermute(block, axis, shift(2, 1))


def order(mine, theirs, axis):
    first = lax.axis_index(axis) == 0
    return jnp.stack([jnp.where(first, mine, theirs), jnp.where(first, theirs, mine)])


def solution(mesh):
    aux, row, col = (mesh.shape[name] for name in ("aux", "row", "col"))
    z2, z1, y, zh, core = 2, aux // 8, 4, col // 2, 2
    zl = z2 * z1
    names = ("z2", "z1", "y", "row", "zh", "core")
    fine = Mesh(mesh.devices.reshape(z2, z1, y, row, zh, core), names)
    line = ("z2", "z1")

    def local(g_plus, g_minus, coulomb):
        count, rows, n = coulomb.shape
        depth, cols = g_minus.shape
        thin = g_plus.shape[1]
        slabs = spread(jnp.concatenate([g_minus, g_plus.T]), line, zl)
        minus, plus = slabs[:, :depth], slabs[:, depth:]
        theirs = partner(plus, "zh")
        minus = spread(minus, ("y", "row"), y * row)
        minus, plus, theirs = lax.optimization_barrier((minus, plus, theirs))
        minus = minus.reshape(y, row, zl, depth, cols).transpose(2, 0, 1, 3, 4).reshape(n, cols)
        half = jnp.einsum("qik,kj->qij", coulomb, minus, preferred_element_type=F32).astype(BF)
        half = with_layout_constraint(half, Layout((0, 1, 2)))

        plus = spread(order(plus, theirs, "zh"), "y", y)
        plus = order(plus, partner(plus, "core"), "core")
        plus = plus.reshape(core, y, zh, zl, thin, rows).transpose(3, 1, 2, 0, 4, 5).reshape(n, rows)

        me = lax.axis_index("row")
        left = lax.ppermute(half, "row", shift(row, 1))
        right = lax.ppermute(half, "row", shift(row, -1))
        cut = rows // 2
        top = lax.ppermute(left[:, :cut], "row", shift(row, 1))
        bottom = lax.ppermute(right[:, cut:], "row", shift(row, -1))

        def part(strip, owner, start):
            size = strip.shape[1]
            block = lax.dynamic_slice_in_dim(plus, owner * rows + start, size, axis=0)
            return jnp.einsum("ki,qkj->qij", block, strip, preferred_element_type=F32)

        pair = part(half, me, 0)
        pair += part(left, (me + row - 1) % row, 0)
        pair += part(right, (me + 1) % row, 0)
        pair += part(top, (me + 2) % row, 0)
        pair += part(bottom, (me + 2) % row, cut)
        total = jnp.sum(pair * half.astype(F32), axis=0)

        parts = y * z1
        total = lax.all_to_all(total.astype(BF).reshape(parts, rows // parts, cols), ("y", "z1"), 0, 0)
        total = jnp.sum(total.astype(F32), axis=0)
        total = -(total + partner(total, "z2"))
        return spread(total.astype(BF), ("y", "z1"), parts).reshape(rows, cols)

    in_specs = (
        P("row", ("z2", "z1", "y", "zh", "core")),
        P(("z2", "z1", "y", "row"), ("zh", "core")),
        P(("z2", "z1", "y"), "row", None),
    )
    out_specs = P("row", ("zh", "core"))
    return jax.shard_map(local, mesh=fine, in_specs=in_specs, out_specs=out_specs, check_vma=False)
```

```python
import jax
import jax.numpy as jnp
from jax import lax
from jax.experimental.layout import Layout, with_layout_constraint
from jax.sharding import Mesh, PartitionSpec as P

BF = jnp.bfloat16
F32 = jnp.float32


def spread(block, axes, count):
    return lax.all_to_all(jnp.broadcast_to(block[None], (count,) + block.shape), axes, 0, 0)


def shift(count, by):
    return [(index, (index + by) % count) for index in range(count)]


def partner(block, axis):
    return lax.ppermute(block, axis, shift(2, 1))


def order(mine, theirs, axis):
    first = lax.axis_index(axis) == 0
    return jnp.stack([jnp.where(first, mine, theirs), jnp.where(first, theirs, mine)])


def solution(mesh):
    aux, row, col = (mesh.shape[name] for name in ("aux", "row", "col"))
    z2, z1, y, zh, core = aux // 8, 2, 4, col // 2, 2
    zl = z2 * z1
    names = ("z2", "z1", "y", "row", "zh", "core")
    fine = Mesh(mesh.devices.reshape(z2, z1, y, row, zh, core), names)
    line = ("z2", "z1")

    def local(g_plus, g_minus, coulomb):
        count, rows, n = coulomb.shape
        depth, cols = g_minus.shape
        thin = g_plus.shape[1]
        slabs = spread(jnp.concatenate([g_minus, g_plus.T]), line, zl)
        minus, plus = slabs[:, :depth], slabs[:, depth:]
        theirs = partner(plus, "zh")
        minus = spread(minus, ("y", "row"), y * row)
        minus, plus, theirs = lax.optimization_barrier((minus, plus, theirs))
        minus = minus.reshape(y, row, zl, depth, cols).transpose(2, 0, 1, 3, 4).reshape(n, cols)
        half = jnp.einsum("qik,kj->qij", coulomb, minus, preferred_element_type=F32).astype(BF)
        half = with_layout_constraint(half, Layout((0, 1, 2)))

        plus = spread(order(plus, theirs, "zh"), "y", y)
        plus = order(plus, partner(plus, "core"), "core")
        plus = plus.reshape(core, y, zh, zl, thin, rows).transpose(3, 1, 2, 0, 4, 5).reshape(n, rows)

        me = lax.axis_index("row")
        left = lax.ppermute(half, "row", shift(row, 1))
        right = lax.ppermute(half, "row", shift(row, -1))
        cut = rows // 2
        top = lax.ppermute(left[:, :cut], "row", shift(row, 1))
        bottom = lax.ppermute(right[:, cut:], "row", shift(row, -1))

        def part(strip, owner, start):
            size = strip.shape[1]
            block = lax.dynamic_slice_in_dim(plus, owner * rows + start, size, axis=0)
            return jnp.einsum("ki,qkj->qij", block, strip, preferred_element_type=F32)

        pair = part(half, me, 0)
        pair += part(left, (me + row - 1) % row, 0)
        pair += part(right, (me + 1) % row, 0)
        pair += part(top, (me + 2) % row, 0)
        pair += part(bottom, (me + 2) % row, cut)
        total = jnp.sum(pair * half.astype(F32), axis=0)

        parts = y * z1
        total = lax.all_to_all(total.astype(BF).reshape(parts, rows // parts, cols), ("y", "z1"), 0, 0)
        total = jnp.sum(total.astype(F32), axis=0).astype(BF)
        total = -jnp.sum(spread(total, "z2", z2).astype(F32), axis=0)
        return spread(total.astype(BF), ("y", "z1"), parts).reshape(rows, cols)

    in_specs = (
        P("row", ("z2", "z1", "y", "zh", "core")),
        P(("z2", "z1", "y", "row"), ("zh", "core")),
        P(("z2", "z1", "y"), "row", None),
    )
    out_specs = P("row", ("zh", "core"))
    return jax.shard_map(local, mesh=fine, in_specs=in_specs, out_specs=out_specs, check_vma=False)
```

```python
import jax
import jax.numpy as jnp
from jax import lax
from jax.experimental.layout import Layout, with_layout_constraint
from jax.sharding import Mesh, PartitionSpec as P

BF = jnp.bfloat16
F32 = jnp.float32


def spread(block, axes, count):
    return lax.all_to_all(jnp.broadcast_to(block[None], (count,) + block.shape), axes, 0, 0)


def shift(count, by):
    return [(index, (index + by) % count) for index in range(count)]


def partner(block, axis):
    return lax.ppermute(block, axis, shift(2, 1))


def order(mine, theirs, axis):
    first = lax.axis_index(axis) == 0
    return jnp.stack([jnp.where(first, mine, theirs), jnp.where(first, theirs, mine)])


def solution(mesh):
    aux, row, col = (mesh.shape[name] for name in ("aux", "row", "col"))
    z2, z1, y, zh, core = aux // 8, 2, 4, col // 2, 2
    names = ("z2", "z1", "y", "row", "zh", "core")
    fine = Mesh(mesh.devices.reshape(z2, z1, y, row, zh, core), names)

    def local(g_plus, g_minus, coulomb):
        count, rows, n = coulomb.shape
        depth, cols = g_minus.shape
        thin = g_plus.shape[1]
        slabs = spread(jnp.concatenate([g_minus, g_plus.T]), "z2", z2)
        minus, plus = slabs[:, :depth], slabs[:, depth:]
        theirs = partner(plus, "zh")
        minus = spread(minus, ("y", "z1"), y * z1)
        minus, plus, theirs = lax.optimization_barrier((minus, plus, theirs))
        minus, plus = lax.optimization_barrier((minus, order(plus, theirs, "zh")))
        minus = spread(minus, "row", row)
        minus, plus = lax.optimization_barrier((minus, plus))
        minus = minus.reshape(row, y, z1, z2, depth, cols).transpose(3, 2, 1, 0, 4, 5).reshape(n, cols)
        half = jnp.einsum("qik,kj->qij", coulomb, minus, preferred_element_type=F32).astype(BF)
        half = with_layout_constraint(half, Layout((0, 1, 2)))

        plus = spread(plus, ("y", "z1"), y * z1)
        plus = order(plus, partner(plus, "core"), "core")
        plus = plus.reshape(core, y, z1, zh, z2, thin, rows).transpose(4, 2, 1, 3, 0, 5, 6).reshape(n, rows)

        me = lax.axis_index("row")
        left = lax.ppermute(half, "row", shift(row, 1))
        right = lax.ppermute(half, "row", shift(row, -1))
        cut = rows // 2
        top = lax.ppermute(left[:, :cut], "row", shift(row, 1))
        bottom = lax.ppermute(right[:, cut:], "row", shift(row, -1))

        def part(strip, owner, start):
            size = strip.shape[1]
            block = lax.dynamic_slice_in_dim(plus, owner * rows + start, size, axis=0)
            return jnp.einsum("ki,qkj->qij", block, strip, preferred_element_type=F32)

        pair = part(half, me, 0)
        pair += part(left, (me + row - 1) % row, 0)
        pair += part(right, (me + 1) % row, 0)
        pair += part(top, (me + 2) % row, 0)
        pair += part(bottom, (me + 2) % row, cut)
        total = jnp.sum(pair * half.astype(F32), axis=0)

        parts = y * z1
        total = lax.all_to_all(total.astype(BF).reshape(parts, rows // parts, cols), ("y", "z1"), 0, 0)
        total = jnp.sum(total.astype(F32), axis=0).astype(BF)
        total = -jnp.sum(spread(total, "z2", z2).astype(F32), axis=0)
        return spread(total.astype(BF), ("y", "z1"), parts).reshape(rows, cols)

    in_specs = (
        P("row", ("z2", "z1", "y", "zh", "core")),
        P(("z2", "z1", "y", "row"), ("zh", "core")),
        P(("z2", "z1", "y"), "row", None),
    )
    out_specs = P("row", ("zh", "core"))
    return jax.shard_map(local, mesh=fine, in_specs=in_specs, out_specs=out_specs, check_vma=False)
```

```python
import jax
import jax.numpy as jnp
from jax import lax
from jax.experimental.layout import Layout, with_layout_constraint
from jax.sharding import Mesh, PartitionSpec as P

BF = jnp.bfloat16
F32 = jnp.float32


def spread(block, axes, count):
    return lax.all_to_all(jnp.broadcast_to(block[None], (count,) + block.shape), axes, 0, 0)


def shift(count, by):
    return [(index, (index + by) % count) for index in range(count)]


def partner(block, axis):
    return lax.ppermute(block, axis, shift(2, 1))


def order(mine, theirs, axis):
    first = lax.axis_index(axis) == 0
    return jnp.stack([jnp.where(first, mine, theirs), jnp.where(first, theirs, mine)])


def solution(mesh):
    aux, row, col = (mesh.shape[name] for name in ("aux", "row", "col"))
    z2, z1, y, zh, core = aux // 8, 2, 4, col // 2, 2
    zl = z2 * z1
    names = ("z2", "z1", "y", "row", "zh", "core")
    fine = Mesh(mesh.devices.reshape(z2, z1, y, row, zh, core), names)
    line = ("z2", "z1")

    def local(g_plus, g_minus, coulomb):
        count, rows, n = coulomb.shape
        depth, cols = g_minus.shape
        thin = g_plus.shape[1]
        slabs = spread(jnp.concatenate([g_minus, g_plus.T]), line, zl)
        minus, plus = slabs[:, :depth], slabs[:, depth:]
        theirs = partner(plus, "zh")
        minus = spread(minus, ("row", "y"), y * row)
        minus, plus, theirs = lax.optimization_barrier((minus, plus, theirs))
        minus = minus.reshape(row, y, zl, depth, cols).transpose(2, 1, 0, 3, 4).reshape(n, cols)
        half = jnp.einsum("qik,kj->qij", coulomb, minus, preferred_element_type=F32).astype(BF)
        half = with_layout_constraint(half, Layout((0, 1, 2)))

        plus = spread(order(plus, theirs, "zh"), "y", y)
        plus = order(plus, partner(plus, "core"), "core")
        plus = plus.reshape(core, y, zh, zl, thin, rows).transpose(3, 1, 2, 0, 4, 5).reshape(n, rows)

        me = lax.axis_index("row")
        left = lax.ppermute(half, "row", shift(row, 1))
        right = lax.ppermute(half, "row", shift(row, -1))
        cut = rows // 2
        top = lax.ppermute(left[:, :cut], "row", shift(row, 1))
        bottom = lax.ppermute(right[:, cut:], "row", shift(row, -1))

        def part(strip, owner, start):
            size = strip.shape[1]
            block = lax.dynamic_slice_in_dim(plus, owner * rows + start, size, axis=0)
            return jnp.einsum("ki,qkj->qij", block, strip, preferred_element_type=F32)

        pair = part(half, me, 0)
        pair += part(left, (me + row - 1) % row, 0)
        pair += part(right, (me + 1) % row, 0)
        pair += part(top, (me + 2) % row, 0)
        pair += part(bottom, (me + 2) % row, cut)
        total = jnp.sum(pair * half.astype(F32), axis=0)

        parts = y * z1
        total = lax.all_to_all(total.astype(BF).reshape(parts, rows // parts, cols), ("z1", "y"), 0, 0)
        total = jnp.sum(total.astype(F32), axis=0).astype(BF)
        total = -jnp.sum(spread(total, "z2", z2).astype(F32), axis=0)
        return spread(total.astype(BF), ("z1", "y"), parts).reshape(rows, cols)

    in_specs = (
        P("row", ("z2", "z1", "y", "zh", "core")),
        P(("z2", "z1", "y", "row"), ("zh", "core")),
        P(("z2", "z1", "y"), "row", None),
    )
    out_specs = P("row", ("zh", "core"))
    return jax.shard_map(local, mesh=fine, in_specs=in_specs, out_specs=out_specs, check_vma=False)
```

```python
import jax
import jax.numpy as jnp
from jax import lax
from jax.experimental.layout import Layout, with_layout_constraint
from jax.sharding import Mesh, PartitionSpec as P

BF = jnp.bfloat16
F32 = jnp.float32


def spread(block, axes, count):
    return lax.all_to_all(jnp.broadcast_to(block[None], (count,) + block.shape), axes, 0, 0)


def shift(count, by):
    return [(index, (index + by) % count) for index in range(count)]


def partner(block, axis):
    return lax.ppermute(block, axis, shift(2, 1))


def order(mine, theirs, axis):
    first = lax.axis_index(axis) == 0
    return jnp.stack([jnp.where(first, mine, theirs), jnp.where(first, theirs, mine)])


def solution(mesh):
    aux, row, col = (mesh.shape[name] for name in ("aux", "row", "col"))
    z2, z1, y, zh, core = aux // 8, 2, 4, col // 2, 2
    zl = z2 * z1
    names = ("z2", "z1", "y", "row", "zh", "core")
    fine = Mesh(mesh.devices.reshape(z2, z1, y, row, zh, core), names)
    line = ("z2", "z1")

    def local(g_plus, g_minus, coulomb):
        count, rows, n = coulomb.shape
        depth, cols = g_minus.shape
        thin = g_plus.shape[1]
        slabs = spread(jnp.concatenate([g_minus, g_plus.T]), line, zl)
        minus, plus = slabs[:, :depth], slabs[:, depth:]
        theirs = partner(plus, "zh")
        minus = spread(minus, ("row", "y"), y * row)
        minus, plus, theirs = lax.optimization_barrier((minus, plus, theirs))
        minus = minus.reshape(row, y, zl, depth, cols).transpose(2, 1, 0, 3, 4).reshape(n, cols)
        half = jnp.einsum("qik,kj->qij", coulomb, minus, preferred_element_type=F32).astype(BF)
        half = with_layout_constraint(half, Layout((0, 1, 2)))

        plus = spread(order(plus, theirs, "zh"), "y", y)
        plus = order(plus, partner(plus, "core"), "core")
        plus = plus.reshape(core, y, zh, zl, thin, rows).transpose(3, 1, 2, 0, 4, 5).reshape(n, rows)

        me = lax.axis_index("row")
        left = lax.ppermute(half, "row", shift(row, 1))
        right = lax.ppermute(half, "row", shift(row, -1))
        far0 = lax.ppermute(left[:1], "row", shift(row, 1))
        far1 = lax.ppermute(right[1:], "row", shift(row, -1))

        def part(strip, owner):
            block = lax.dynamic_slice_in_dim(plus, owner * rows, rows, axis=0)
            return jnp.einsum("ki,qkj->qij", block, strip, preferred_element_type=F32)

        pair = part(half, me)
        pair += part(left, (me + row - 1) % row)
        pair += part(right, (me + 1) % row)
        pair += jnp.concatenate([part(far0, (me + 2) % row), part(far1, (me + 2) % row)])
        total = jnp.sum(pair * half.astype(F32), axis=0)

        parts = y * z1
        total = lax.all_to_all(total.astype(BF).reshape(parts, rows // parts, cols), ("z1", "y"), 0, 0)
        total = jnp.sum(total.astype(F32), axis=0).astype(BF)
        total = -jnp.sum(spread(total, "z2", z2).astype(F32), axis=0)
        return spread(total.astype(BF), ("z1", "y"), parts).reshape(rows, cols)

    in_specs = (
        P("row", ("z2", "z1", "y", "zh", "core")),
        P(("z2", "z1", "y", "row"), ("zh", "core")),
        P(("z2", "z1", "y"), "row", None),
    )
    out_specs = P("row", ("zh", "core"))
    return jax.shard_map(local, mesh=fine, in_specs=in_specs, out_specs=out_specs, check_vma=False)
```

```python
import jax
import jax.numpy as jnp
from jax import lax
from jax.experimental.layout import Layout, with_layout_constraint
from jax.sharding import Mesh, PartitionSpec as P

BF = jnp.bfloat16
F32 = jnp.float32


def spread(block, axes, count):
    return lax.all_to_all(jnp.broadcast_to(block[None], (count,) + block.shape), axes, 0, 0)


def shift(count, by):
    return [(index, (index + by) % count) for index in range(count)]


def partner(block, axis):
    return lax.ppermute(block, axis, shift(2, 1))


def order(mine, theirs, axis):
    first = lax.axis_index(axis) == 0
    return jnp.stack([jnp.where(first, mine, theirs), jnp.where(first, theirs, mine)])


def solution(mesh):
    aux, row, col = (mesh.shape[name] for name in ("aux", "row", "col"))
    z2, z1, y, zh, core = aux // 8, 2, 4, col // 2, 2
    zl = z2 * z1
    names = ("z2", "z1", "y", "row", "zh", "core")
    fine = Mesh(mesh.devices.reshape(z2, z1, y, row, zh, core), names)
    line = ("z2", "z1")

    def local(g_plus, g_minus, coulomb):
        count, rows, n = coulomb.shape
        depth, cols = g_minus.shape
        thin = g_plus.shape[1]
        slabs = spread(jnp.concatenate([g_minus, g_plus.T]), line, zl)
        minus, plus = slabs[:, :depth], slabs[:, depth:]
        last = zl * zh - 1
        theirs = lax.ppermute(plus, ("z2", "z1", "zh"), [(at, last - at) for at in range(zl * zh)])
        minus = spread(minus, ("row", "y"), y * row)
        minus, plus, theirs = lax.optimization_barrier((minus, plus, theirs))
        minus = minus.reshape(row, y, zl, depth, cols).transpose(2, 1, 0, 3, 4).reshape(n, cols)
        half = jnp.einsum("qik,kj->qij", coulomb, minus, preferred_element_type=F32).astype(BF)
        half = with_layout_constraint(half, Layout((0, 1, 2)))

        plus = spread(order(plus, theirs, "zh"), "y", y)
        plus = order(plus, partner(plus, "core"), "core")
        plus = plus.reshape(core, y, zh, zl, thin, rows).transpose(3, 1, 2, 0, 4, 5).reshape(n, rows)

        me = lax.axis_index("row")
        left = lax.ppermute(half, "row", shift(row, 1))
        right = lax.ppermute(half, "row", shift(row, -1))
        cut = rows // 2
        top = lax.ppermute(left[:, :cut], "row", shift(row, 1))
        bottom = lax.ppermute(right[:, cut:], "row", shift(row, -1))

        def part(strip, owner, start):
            size = strip.shape[1]
            block = lax.dynamic_slice_in_dim(plus, owner * rows + start, size, axis=0)
            return jnp.einsum("ki,qkj->qij", block, strip, preferred_element_type=F32)

        pair = part(half, me, 0)
        pair += part(left, (me + row - 1) % row, 0)
        pair += part(right, (me + 1) % row, 0)
        pair += part(top, (me + 2) % row, 0)
        pair += part(bottom, (me + 2) % row, cut)
        total = jnp.sum(pair * half.astype(F32), axis=0)

        parts = y * z1
        total = lax.all_to_all(total.astype(BF).reshape(parts, rows // parts, cols), ("z1", "y"), 0, 0)
        total = jnp.sum(total.astype(F32), axis=0).astype(BF)
        total = -jnp.sum(spread(total, "z2", z2).astype(F32), axis=0)
        return spread(total.astype(BF), ("z1", "y"), parts).reshape(rows, cols)

    in_specs = (
        P("row", ("z2", "z1", "y", "zh", "core")),
        P(("z2", "z1", "y", "row"), ("zh", "core")),
        P(("z2", "z1", "y"), "row", None),
    )
    out_specs = P("row", ("zh", "core"))
    return jax.shard_map(local, mesh=fine, in_specs=in_specs, out_specs=out_specs, check_vma=False)
```
